32 devices in a mesh: groups: 2 (over y), corr: 16 (over z, x, core).
Axes of the slice: x: 2, y: 2, z: 4, core: 2. Of those that a mesh axis runs over, the one named last changes fastest.
Arguments:
- patterns: bfloat16 [256, 256, 256], P(('groups', 'corr')), parts along dimension 0, may hold values from -6 to 6
- templates: bfloat16 [16, 23040], P('corr'), may hold values from -6 to 6
- sample_pixels: int32 [23040], replicated, may hold values from 0 to 65278, as said below
- fractions: float32 [2, 23040], replicated, may hold values from 0 to 1
Outputs:
- smoothed: bfloat16 [256, 23040], P(('groups', 'corr')), parts along dimension 0
- best: float32 [256], P(('groups', 'corr')), parts along dimension 0
The draws below stay inside these ranges and needn't reach their ends.
There are 2 independent parts, one for each index of `groups`. The reference program is written for one: setup_inputs(seed, part) draws one part's arguments, and reference() takes and returns one part's arrays. A program takes and returns all parts, laid end to end along the dimension named above; an argument that names none is the same for every part. Nothing has to cross between parts.
Inputs may be any that keep to these rules, and one draw needn't show every extreme that they name: `sample_pixels`: each entry is 256 r + c with r and c from 0 to 254.
All inputs are finite; a program needn't handle non-finite values.
Results may differ from the reference program's by a relative error of at most 0.0063.
Values may be sent and summed in bfloat16 or wider, within the bound.
A program may use at most 128 MiB of HBM per device.

```python
import math
import jax
import jax.numpy as jnp
from jax import lax

DET = 256
RADII = 64
ANGLES = 360
PAT_DEV = 8
FREQ = 181
PATTERNS = 128
TEMPL = 16
N_CORR = 16


def draw_sample_pixels(key, part):
    row_key, col_key = jax.random.split(jax.random.fold_in(key, 11))
    row_ids = jax.random.randint(row_key, (RADII * ANGLES,), 0, DET - 1)
    col_ids = jax.random.randint(col_key, (RADII * ANGLES,), 0, DET - 1)
    pixels = (row_ids * DET + col_ids).astype(jnp.int32)
    pixels = pixels.at[0].set((DET - 2) * DET + DET - 2)
    pixels = pixels.at[1].set(0)
    return pixels


def shard_levels(key, extent, shards, least, largest):
    def one(axis_at, blocks):
        steps = jax.random.uniform(jax.random.fold_in(jax.random.fold_in(key, 6), axis_at), (blocks,), jnp.float32, least / len(shards), largest / len(shards))
        return jnp.repeat(jnp.exp(steps), extent[axis_at] // blocks).reshape((-1,) + (1,) * (len(extent) - axis_at - 1))

    factor_of = one(*shards[0])
    for cut in shards[1:]:
        factor_of = factor_of * one(*cut)
    return factor_of


def normal_values(own_key, dims, deviation, bound, pieces=(), kind=jnp.bfloat16):
    level = shard_levels(own_key, dims, pieces, -0.22, 0.18) if pieces else 1.0
    entries = jax.random.normal(own_key, dims, jnp.float32) * deviation * level
    return jnp.minimum(jnp.maximum(entries, -bound), bound).astype(kind)


def setup_inputs(seed: int = 0, part: int = 0) -> dict:
    splits = jax.random.split(jax.random.key(seed), 5)
    part_keys = jax.random.split(jax.random.fold_in(splits[4], part), 5)
    patterns = normal_values(part_keys[0], (PATTERNS, DET, DET), 1.0, 6.0, ((0, 16),))
    templates = normal_values(splits[1], (TEMPL, RADII * ANGLES), 1.0, 6.0, ((0, 16),))
    sample_pixels = draw_sample_pixels(jax.random.fold_in(splits[4], 71), part)
    fractions = jnp.clip(jax.random.uniform(splits[3], (2, RADII * ANGLES), jnp.float32, 0.0, 1.0), 0.0, 1.0)
    return dict(patterns=patterns, templates=templates, sample_pixels=sample_pixels, fractions=fractions)


kernel_sigma = 1.5

def kernels(size):
    offset = (jnp.arange(size)[:, None] - jnp.arange(size)[None, :]).astype(jnp.float32)
    squared = offset * offset
    bell_kernel = jnp.exp(-squared / (2.0 * kernel_sigma ** 2)) / (math.sqrt(2.0 * math.pi) * kernel_sigma)
    curve_kernel = (squared / kernel_sigma ** 4 - 1.0 / kernel_sigma ** 2) * bell_kernel
    return (bell_kernel.astype(jnp.bfloat16), curve_kernel.astype(jnp.bfloat16))

def filter_block(pattern_block, bell_kernel, curve_kernel, sample_pixels, fractions):
    widened = pattern_block.astype(jnp.float32)
    bell_wide = bell_kernel.astype(jnp.float32)
    curve_wide = curve_kernel.astype(jnp.float32)
    left_bell = jnp.einsum('bij,jk->bik', widened, bell_wide).astype(jnp.bfloat16)
    left_curve = jnp.einsum('bij,jk->bik', widened, curve_wide).astype(jnp.bfloat16)
    left_bell = lax.optimization_barrier(left_bell).astype(jnp.float32)
    left_curve = lax.optimization_barrier(left_curve).astype(jnp.float32)
    filtered = jnp.einsum('ij,bjk->bik', curve_wide, left_bell) + jnp.einsum('ij,bjk->bik', bell_wide, left_curve)
    flattened = filtered.reshape(filtered.shape[0], DET * DET)
    across = fractions[0]
    downward = fractions[1]
    polar_rows = (1.0 - across) * (1.0 - downward) * jnp.take(flattened, sample_pixels, axis=1) + across * (1.0 - downward) * jnp.take(flattened, sample_pixels + 1, axis=1) + (1.0 - across) * downward * jnp.take(flattened, sample_pixels + DET, axis=1) + across * downward * jnp.take(flattened, sample_pixels + DET + 1, axis=1)
    return polar_rows.astype(jnp.bfloat16)

def reference(patterns, templates, sample_pixels, fractions):
    bell_kernel, curve_kernel = kernels(DET)
    grouped = patterns.reshape(N_CORR, PAT_DEV, DET, DET)
    polar_rows = lax.map(lambda pattern_block: filter_block(pattern_block, bell_kernel, curve_kernel, sample_pixels, fractions), grouped)
    polar_rows = lax.optimization_barrier(polar_rows.reshape(PATTERNS, RADII * ANGLES)).astype(jnp.float32)
    padded = jnp.pad(polar_rows, ((1, 1), (0, 0)))
    smoothed = ((padded[:-2] + 2.0 * padded[1:-1] + padded[2:]) * 0.25).astype(jnp.bfloat16)
    smooth_wide = lax.optimization_barrier(smoothed).astype(jnp.float32)
    pattern_norm = jnp.sqrt(lax.optimization_barrier(jnp.sum(smooth_wide * smooth_wide, axis=1)) + 1e-06)
    templ_wide = templates.astype(jnp.float32)
    templ_norm = jnp.sqrt(lax.optimization_barrier(jnp.sum(templ_wide * templ_wide, axis=1)) + 1e-06)
    templ_spec = jnp.fft.rfft(templ_wide.reshape(TEMPL, RADII, ANGLES), axis=-1)
    pattern_spec = jnp.fft.rfft(smooth_wide.reshape(PATTERNS, RADII, ANGLES), axis=-1)

    def block_best(spec_block):
        cross = jnp.einsum('prk,trk->ptk', jnp.conj(spec_block), templ_spec)
        shifted = jnp.fft.irfft(cross, n=ANGLES, axis=-1)
        return lax.optimization_barrier(jnp.max(shifted / templ_norm[None, :, None], axis=(1, 2)))
    raw_best = lax.map(block_best, pattern_spec.reshape(N_CORR, PAT_DEV, RADII, FREQ)).reshape(PATTERNS)
    best = raw_best * math.sqrt(RADII * ANGLES) / pattern_norm
    return (smoothed, best)
```

```python
import functools
import math

import jax
import jax.numpy as jnp
import ml_dtypes
import numpy as np
from jax import lax
from jax.experimental import pallas as pl
from jax.experimental.pallas import tpu as pltpu
from jax.sharding import PartitionSpec as P

RADII = 64
ANGLES = 360
FREQ = 181
SIGMA = 1.5
WIDE = 384
HALF = 256
CHUNK = 256
VMEM = pl.BlockSpec(memory_space=pltpu.VMEM)


def filter_tables(size):
    ids = np.arange(size)
    squared = ((ids[:, None] - ids[None, :]) ** 2).astype(np.float32)
    bell = np.exp(-squared / np.float32(2 * SIGMA**2)) / np.float32(math.sqrt(2 * math.pi) * SIGMA)
    curve = (squared / np.float32(SIGMA**4) - np.float32(1 / SIGMA**2)) * bell
    bell, curve = bell.astype(ml_dtypes.bfloat16), curve.astype(ml_dtypes.bfloat16)
    return np.concatenate([bell, curve], axis=1), np.concatenate([curve, bell], axis=1)


def split(table):
    high = table.astype(ml_dtypes.bfloat16)
    low = (table - high.astype(np.float64)).astype(ml_dtypes.bfloat16)
    return np.concatenate([high, low], axis=1)


def dft_tables():
    phase = np.outer(np.arange(ANGLES), np.arange(FREQ)) % ANGLES * (2 * math.pi / ANGLES)
    forward = np.zeros((WIDE, 2 * HALF))
    forward[:ANGLES, :FREQ] = np.cos(phase)
    forward[:ANGLES, HALF : HALF + FREQ] = -np.sin(phase)
    factor = np.full((FREQ, 1), 2.0 / ANGLES)
    factor[0] = factor[FREQ - 1] = 1.0 / ANGLES
    inverse = np.zeros((2 * HALF, WIDE))
    inverse[:FREQ, :ANGLES] = np.cos(phase).T * factor
    inverse[HALF : HALF + FREQ, :ANGLES] = -np.sin(phase).T * factor
    inverse[:, ANGLES:] = inverse[:, :1]
    return split(forward), inverse.astype(np.float32)


def pick(rows, masks):
    for mask in masks:
        rows = [jnp.where(mask, rows[i + 1], rows[i]) for i in range(0, len(rows), 2)]
    return rows[0]


def pick_tree(get, masks, level, at):
    if level == 0:
        return get(at)
    low = pick_tree(get, masks, level - 1, at)
    high = pick_tree(get, masks, level - 1, at + (1 << (level - 1)))
    return jnp.where(masks[level - 1], high, low)


def sample_kernel(pat_ref, first_ref, second_ref, pix_ref, frac_ref, polar_ref, wide_ref, rows_ref):
    count, side = pat_ref.shape[0], pat_ref.shape[1]
    for p in range(count):
        left = jnp.dot(pat_ref[p], first_ref[...], preferred_element_type=jnp.float32)
        left = left.astype(jnp.bfloat16)
        left = jnp.concatenate([left[:, :side], left[:, side:]], axis=0)
        filtered = jnp.dot(second_ref[...], left, preferred_element_type=jnp.float32)
        wide_ref[:, p, :] = filtered
    rows_ref[...] = wide_ref[...].reshape(side * count, side).astype(jnp.bfloat16)

    @pl.loop(0, pix_ref.shape[1] // CHUNK)
    def _(step):
        at = pl.ds(pl.multiple_of(step * CHUNK, CHUNK), CHUNK)
        pixel = pix_ref[:, at]
        across = frac_ref[0:1, at]
        downward = jnp.broadcast_to(frac_ref[1:2, at], (count, CHUNK))
        col = pixel & (side - 1)
        row = jnp.broadcast_to(pixel >> 8, (count, CHUNK))
        ids = lax.broadcasted_iota(jnp.int32, (side, CHUNK), 0)
        weights = jnp.where(
            ids == col, 1.0 - across, jnp.where(ids == col + 1, across, 0.0)
        ).astype(jnp.bfloat16)
        taken = jnp.dot(rows_ref[...], weights, preferred_element_type=jnp.float32)
        bits = side.bit_length() - 2
        even_at, odd_at = (row + 1) >> 1, row >> 1
        even_masks = [(even_at & (1 << b)) != 0 for b in range(bits)]
        odd_masks = [(odd_at & (1 << b)) != 0 for b in range(bits)]

        def row_of(r):
            return taken[r * count : (r + 1) * count]

        even = pick_tree(lambda i: row_of(2 * i), even_masks, bits, 0)
        odd = pick_tree(lambda i: row_of(2 * i + 1), odd_masks, bits, 0)
        is_odd = (row & 1) != 0
        top = jnp.where(is_odd, odd, even)
        bottom = jnp.where(is_odd, even, odd)
        polar = (1.0 - downward) * top + downward * bottom
        polar_ref[:, at] = polar.astype(jnp.bfloat16)


def match_kernel(
    polar_ref, low_ref, high_ref, templ_ref, fwd_ref, inv_ref, smooth_ref, best_ref,
    padded_ref, line_ref, spec_ref, templ_spec_ref, norm_ref, cross_ref,
):
    count, width = polar_ref.shape
    number = templ_ref.shape[0] // RADII
    block = 1152
    ids = lax.broadcasted_iota(jnp.int32, (count, block), 0)
    total = jnp.zeros((count, 128), jnp.float32)
    for start in range(0, width, block):
        at = pl.ds(start, block)
        rows = polar_ref[:, at].astype(jnp.float32)
        low = jnp.broadcast_to(low_ref[:, at].astype(jnp.float32), rows.shape)
        high = jnp.broadcast_to(high_ref[:, at].astype(jnp.float32), rows.shape)
        before = jnp.where(ids == 0, low, pltpu.roll(rows, 1, 0))
        after = jnp.where(ids == count - 1, high, pltpu.roll(rows, count - 1, 0))
        smooth = ((before + 2.0 * rows + after) * 0.25).astype(jnp.bfloat16)
        smooth_ref[:, at] = smooth
        smooth = smooth.astype(jnp.float32)
        padded_ref[:, at] = smooth
        squares = smooth * smooth
        for lane in range(0, block, 128):
            total = total + squares[:, lane : lane + 128]
    pattern_norm = jnp.sqrt(jnp.sum(total, axis=1, keepdims=True) + 1e-06)
    padded_ref[:, width:] = jnp.zeros((count, padded_ref.shape[1] - width), jnp.float32)

    real_lane = lax.broadcasted_iota(jnp.int32, (count, WIDE), 1) < ANGLES
    for r in range(RADII):
        start = r * ANGLES
        base = start // 128 * 128
        window = padded_ref[:, base : base + 512]
        if start > base:
            window = pltpu.roll(window, 512 - (start - base), 1)
        line_ref[r * count : (r + 1) * count, :] = jnp.where(real_lane, window[:, :WIDE], 0.0)

    def spectrum(lines):
        both = jnp.dot(lines, fwd_ref[...], preferred_element_type=jnp.float32)
        return both[:, : 2 * HALF] + both[:, 2 * HALF :]

    spec_ref[...] = spectrum(line_ref[...].astype(jnp.bfloat16))

    @pl.loop(0, number)
    def _(t):
        at = pl.ds(pl.multiple_of(t * RADII, RADII), RADII)
        lines = templ_ref[at, :]
        templ_spec_ref[at, :] = spectrum(lines)
        lines = lines.astype(jnp.float32)
        norm = jnp.sqrt(jnp.sum(lines * lines, keepdims=True) + 1e-06)
        real = [jnp.zeros((count, HALF), jnp.float32)] * 1
        imag = [jnp.zeros((count, HALF), jnp.float32)] * 1
        real, imag = real[0], imag[0]
        for r in range(RADII):
            pat = spec_ref[r * count : (r + 1) * count, :]
            tem = templ_spec_ref[pl.ds(t * RADII + r, 1), :]
            pr, pi, tr, ti = pat[:, :HALF], pat[:, HALF:], tem[:, :HALF], tem[:, HALF:]
            real = real + pr * tr + pi * ti
            imag = imag + pr * ti - pi * tr
        out = pl.ds(pl.multiple_of(t * count, count), count)
        scale = 1.0 / norm
        cross_ref[out, :HALF] = real * scale
        cross_ref[out, HALF:] = imag * scale

    scaled = jnp.dot(
        cross_ref[...], inv_ref[...], precision=lax.Precision.HIGHEST,
        preferred_element_type=jnp.float32,
    )
    top = jnp.max(scaled.reshape(number, count, WIDE), axis=0)
    best = jnp.max(top, axis=1, keepdims=True)
    best = best * math.sqrt(RADII * ANGLES) / pattern_norm
    best_ref[...] = jnp.broadcast_to(best, best_ref.shape)


def body(patterns, templates, pixels, fractions):
    count, side = patterns.shape[0], patterns.shape[1]
    width = pixels.shape[0]
    first, second = filter_tables(side)
    forward, inverse = dft_tables()
    size = lax.axis_size("corr")
    own = templates.reshape(-1, ANGLES)
    own = jnp.pad(own, ((0, 0), (0, WIDE - ANGLES)))
    library = lax.all_gather(own, "corr", axis=0, tiled=True)
    polar = pl.pallas_call(
        sample_kernel,
        out_shape=jax.ShapeDtypeStruct((count, width), jnp.bfloat16),
        in_specs=[VMEM] * 5,
        out_specs=VMEM,
        scratch_shapes=[
            pltpu.VMEM((side, count, side), jnp.float32),
            pltpu.VMEM((side * count, side), jnp.bfloat16),
        ],
        compiler_params=pltpu.CompilerParams(vmem_limit_bytes=40 << 20),
        cost_estimate=pl.CostEstimate(
            flops=2 * count * side * side * width, bytes_accessed=3 << 20, transcendentals=0
        ),
    )(patterns, jnp.asarray(first), jnp.asarray(second), pixels[None], fractions)
    forward_pairs = [(i, i + 1) for i in range(size - 1)]
    backward_pairs = [(i + 1, i) for i in range(size - 1)]
    low = lax.ppermute(polar[count - 1 :], "corr", forward_pairs)
    high = lax.ppermute(polar[:1], "corr", backward_pairs)
    number = library.shape[0] // RADII
    smoothed, best = pl.pallas_call(
        match_kernel,
        out_shape=(
            jax.ShapeDtypeStruct((count, width), jnp.bfloat16),
            jax.ShapeDtypeStruct((count, 128), jnp.float32),
        ),
        in_specs=[VMEM] * 6,
        out_specs=(VMEM, VMEM),
        scratch_shapes=[
            pltpu.VMEM((count, width + 512), jnp.float32),
            pltpu.VMEM((RADII * count, WIDE), jnp.float32),
            pltpu.VMEM((RADII * count, 2 * HALF), jnp.float32),
            pltpu.VMEM((number * RADII, 2 * HALF), jnp.float32),
            pltpu.VMEM((8, 128), jnp.float32),
            pltpu.VMEM((number * count, 2 * HALF), jnp.float32),
        ],
        compiler_params=pltpu.CompilerParams(vmem_limit_bytes=50 << 20),
    )(polar, low, high, library, jnp.asarray(forward), jnp.asarray(inverse))
    return smoothed, best[:, 0]


def solution(mesh):
    in_specs = (P(("groups", "corr"), None, None), P("corr", None), P(), P())
    out_specs = (P(("groups", "corr"), None), P(("groups", "corr")))
    return jax.shard_map(body, mesh=mesh, in_specs=in_specs, out_specs=out_specs, check_vma=False)
```

```python
import functools
import math

import jax
import jax.numpy as jnp
import ml_dtypes
import numpy as np
from jax import lax
from jax.experimental import pallas as pl
from jax.experimental.pallas import tpu as pltpu
from jax.sharding import PartitionSpec as P

RADII = 64
ANGLES = 360
FREQ = 181
SIGMA = 1.5
WIDE = 384
HALF = 256
CHUNK = 256
VMEM = pl.BlockSpec(memory_space=pltpu.VMEM)


def filter_tables(size):
    ids = np.arange(size)
    squared = ((ids[:, None] - ids[None, :]) ** 2).astype(np.float32)
    bell = np.exp(-squared / np.float32(2 * SIGMA**2)) / np.float32(math.sqrt(2 * math.pi) * SIGMA)
    curve = (squared / np.float32(SIGMA**4) - np.float32(1 / SIGMA**2)) * bell
    bell, curve = bell.astype(ml_dtypes.bfloat16), curve.astype(ml_dtypes.bfloat16)
    return np.concatenate([bell, curve], axis=1), np.concatenate([curve, bell], axis=1)


def split(table):
    high = table.astype(ml_dtypes.bfloat16)
    low = (table - high.astype(np.float64)).astype(ml_dtypes.bfloat16)
    return np.concatenate([high, low], axis=1)


def dft_tables():
    phase = np.outer(np.arange(ANGLES), np.arange(FREQ)) % ANGLES * (2 * math.pi / ANGLES)
    forward = np.zeros((WIDE, 2 * HALF))
    forward[:ANGLES, :FREQ] = np.cos(phase)
    forward[:ANGLES, HALF : HALF + FREQ] = -np.sin(phase)
    factor = np.full((FREQ, 1), 2.0 / ANGLES)
    factor[0] = factor[FREQ - 1] = 1.0 / ANGLES
    inverse = np.zeros((2 * HALF, WIDE))
    inverse[:FREQ, :ANGLES] = np.cos(phase).T * factor
    inverse[HALF : HALF + FREQ, :ANGLES] = -np.sin(phase).T * factor
    inverse[:, ANGLES:] = inverse[:, :1]
    return split(forward), inverse.astype(np.float32)


def pick_tree(get, masks, level, at):
    if level == 0:
        return get(at)
    low = pick_tree(get, masks, level - 1, at)
    high = pick_tree(get, masks, level - 1, at + (1 << (level - 1)))
    return jnp.where(masks[level - 1], high, low)


def column_weights(pix_ref, frac_ref, tile, side, out_ref):
    ids = lax.broadcasted_iota(jnp.int32, (side, 128), 0)
    for part in range(CHUNK // 128):
        col = pix_ref[pl.ds(tile + part, 1), :] & (side - 1)
        across = frac_ref[0, pl.ds(tile + part, 1), :]
        weights = jnp.where(ids == col, 1.0 - across, jnp.where(ids == col + 1, across, 0.0))
        out_ref[:, part * 128 : (part + 1) * 128] = weights.astype(jnp.bfloat16)


def sample_step(pix_ref, frac_ref, rows_ref, weights_ref, tile, count, bits):
    taken = jnp.dot(rows_ref[...], weights_ref[...], preferred_element_type=jnp.float32)
    out = []
    for part in range(CHUNK // 128):
        lanes = slice(part * 128, (part + 1) * 128)
        row = jnp.broadcast_to(pix_ref[pl.ds(tile + part, 1), :] >> (bits + 1), (count, 128))
        downward = jnp.broadcast_to(frac_ref[1, pl.ds(tile + part, 1), :], (count, 128))
        even_at, odd_at = (row + 1) >> 1, row >> 1
        even_masks = [(even_at & (1 << b)) != 0 for b in range(bits)]
        odd_masks = [(odd_at & (1 << b)) != 0 for b in range(bits)]

        def row_of(r):
            return taken[r * count : (r + 1) * count, lanes]

        even = pick_tree(lambda i: row_of(2 * i), even_masks, bits, 0)
        odd = pick_tree(lambda i: row_of(2 * i + 1), odd_masks, bits, 0)
        is_odd = (row & 1) != 0
        top = jnp.where(is_odd, odd, even)
        bottom = jnp.where(is_odd, even, odd)
        polar = (1.0 - downward) * top + downward * bottom
        out.append(polar.astype(jnp.bfloat16).astype(jnp.float32))
    return out


def kernel(
    size, pat_hbm, first_hbm, second_hbm, pix_hbm, frac_hbm, templ_hbm, fwd_hbm, inv_hbm,
    smooth_ref, best_ref,
    pat_ref, first_ref, second_ref, pix_ref, frac_ref, templ_ref, fwd_ref, inv_ref,
    wide_ref, rows_ref, even_ref, odd_ref, padded_ref, line_ref, spec_ref, templ_spec_ref,
    cross_ref, library_ref, last_ref, first_row_ref, low_ref, high_ref,
    load_sem, send_sem, recv_sem, halo_send, halo_recv,
):
    me = lax.axis_index("corr")
    loads = [
        pltpu.make_async_copy(source, target, load_sem.at[i])
        for i, (source, target) in enumerate((
            (templ_hbm, templ_ref), (pat_hbm, pat_ref), (first_hbm, first_ref),
            (second_hbm, second_ref), (pix_hbm, pix_ref), (frac_hbm, frac_ref),
            (fwd_hbm, fwd_ref), (inv_hbm, inv_ref),
        ))
    ]
    for load in loads:
        load.start()

    barrier = pltpu.get_barrier_semaphore()

    def partner(k):
        return {"corr": lax.rem(me + k, size)}

    @pl.loop(1, size)
    def _(k):
        pl.semaphore_signal(
            barrier, inc=1, device_id=partner(k), device_id_type=pl.DeviceIdType.MESH
        )

    pl.semaphore_wait(barrier, size - 1)
    loads[0].wait()

    def share(k):
        return pltpu.make_async_remote_copy(
            src_ref=templ_ref,
            dst_ref=library_ref.at[me],
            send_sem=send_sem.at[k],
            recv_sem=recv_sem.at[k],
            device_id=partner(k),
            device_id_type=pl.DeviceIdType.MESH,
        )

    @pl.loop(1, size)
    def _(k):
        share(k).start()

    library_ref[me] = templ_ref[...]

    count, side = pat_ref.shape[0], pat_ref.shape[1]
    bits = side.bit_length() - 2
    tiles = pix_ref.shape[0]
    width = tiles * 128
    for load in loads[1:4]:
        load.wait()
    for p in range(count):
        left = jnp.dot(pat_ref[p], first_ref[...], preferred_element_type=jnp.float32)
        left = left.astype(jnp.bfloat16)
        left = jnp.concatenate([left[:, :side], left[:, side:]], axis=0)
        filtered = jnp.dot(second_ref[...], left, preferred_element_type=jnp.float32)
        wide_ref[:, p, :] = filtered
    rows_ref[...] = wide_ref[...].reshape(side * count, side).astype(jnp.bfloat16)
    loads[4].wait()
    loads[5].wait()

    each = CHUNK // 128
    pairs = tiles // (2 * each)
    column_weights(pix_ref, frac_ref, 0, side, even_ref)

    def keep(tile, rows):
        for part, polar in enumerate(rows):
            padded_ref[tile + part] = polar
            first_row_ref[pl.ds(tile + part, 1), :] = polar[:1]
            last_ref[pl.ds(tile + part, 1), :] = polar[count - 1 :]

    @pl.loop(0, pairs)
    def _(step):
        now = step * (2 * each)
        later = lax.rem(step + 1, pairs) * (2 * each)
        column_weights(pix_ref, frac_ref, now + each, side, odd_ref)
        rows = sample_step(pix_ref, frac_ref, rows_ref, even_ref, now, count, bits)
        column_weights(pix_ref, frac_ref, later, side, even_ref)
        more = sample_step(pix_ref, frac_ref, rows_ref, odd_ref, now + each, count, bits)
        keep(now, rows)
        keep(now + each, more)

    def halo(i, source, target, to):
        return pltpu.make_async_remote_copy(
            src_ref=source,
            dst_ref=target,
            send_sem=halo_send.at[i],
            recv_sem=halo_recv.at[i],
            device_id={"corr": to},
            device_id_type=pl.DeviceIdType.MESH,
        )

    upward = halo(0, last_ref, low_ref, lax.rem(me + 1, size))
    downward = halo(1, first_row_ref, high_ref, lax.rem(me + size - 1, size))
    upward.start()
    downward.start()
    loads[6].wait()
    loads[7].wait()

    @pl.loop(1, size)
    def _(k):
        share(k).wait()

    def spectrum(lines):
        both = jnp.dot(lines, fwd_ref[...], preferred_element_type=jnp.float32)
        return both[:, : 2 * HALF] + both[:, 2 * HALF :]

    @pl.loop(0, size)
    def _(t):
        templ_spec_ref[pl.ds(pl.multiple_of(t * RADII, RADII), RADII), :] = spectrum(library_ref[t])

    upward.wait()
    downward.wait()
    has_low = jnp.where(me > 0, 1.0, 0.0)
    has_high = jnp.where(me < size - 1, 1.0, 0.0)
    ids = lax.broadcasted_iota(jnp.int32, (count, 128), 0)
    total = jnp.zeros((count, 128), jnp.float32)
    for tile in range(tiles):
        rows = padded_ref[tile]
        low = jnp.broadcast_to(low_ref[tile : tile + 1, :], rows.shape) * has_low
        high = jnp.broadcast_to(high_ref[tile : tile + 1, :], rows.shape) * has_high
        before = jnp.where(ids == 0, low, pltpu.roll(rows, 1, 0))
        after = jnp.where(ids == count - 1, high, pltpu.roll(rows, count - 1, 0))
        smooth = ((before + 2.0 * rows + after) * 0.25).astype(jnp.bfloat16)
        smooth_ref[:, tile * 128 : (tile + 1) * 128] = smooth
        smooth = smooth.astype(jnp.float32)
        padded_ref[tile] = smooth
        total = total + smooth * smooth
    pattern_norm = jnp.sqrt(jnp.sum(total, axis=1, keepdims=True) + 1e-06)

    real_lane = lax.broadcasted_iota(jnp.int32, (count, WIDE), 1) < ANGLES
    for r in range(RADII):
        start = r * ANGLES
        base = start // 128
        window = jnp.concatenate([padded_ref[min(base + i, tiles - 1)] for i in range(4)], axis=1)
        if start > base * 128:
            window = pltpu.roll(window, 512 - (start - base * 128), 1)
        line_ref[r * count : (r + 1) * count, :] = jnp.where(real_lane, window[:, :WIDE], 0.0)
    spec_ref[...] = spectrum(line_ref[...].astype(jnp.bfloat16))

    @pl.loop(0, size)
    def _(t):
        lines = library_ref[t].astype(jnp.float32)
        norm = jnp.sqrt(jnp.sum(lines * lines, keepdims=True) + 1e-06)
        real = jnp.zeros((count, HALF), jnp.float32)
        imag = jnp.zeros((count, HALF), jnp.float32)
        for r in range(RADII):
            pat = spec_ref[r * count : (r + 1) * count, :]
            tem = templ_spec_ref[pl.ds(t * RADII + r, 1), :]
            pr, pi, tr, ti = pat[:, :HALF], pat[:, HALF:], tem[:, :HALF], tem[:, HALF:]
            real = real + pr * tr + pi * ti
            imag = imag + pr * ti - pi * tr
        out = pl.ds(pl.multiple_of(t * count, count), count)
        scale = 1.0 / norm
        cross_ref[out, :HALF] = real * scale
        cross_ref[out, HALF:] = imag * scale

    scaled = jnp.dot(
        cross_ref[...], inv_ref[...], precision=lax.Precision.HIGHEST,
        preferred_element_type=jnp.float32,
    )
    top = jnp.max(scaled.reshape(size, count, WIDE), axis=0)
    best = jnp.max(top, axis=1, keepdims=True)
    best = best * math.sqrt(RADII * ANGLES) / pattern_norm
    best_ref[...] = jnp.broadcast_to(best, best_ref.shape)


def body(patterns, templates, pixels, fractions):
    count, side = patterns.shape[0], patterns.shape[1]
    width = pixels.shape[0]
    tiles = width // 128
    first, second = filter_tables(side)
    forward, inverse = dft_tables()
    size = lax.axis_size("corr")
    own = jnp.pad(templates.reshape(-1, ANGLES), ((0, 0), (0, WIDE - ANGLES)))
    operands = (
        patterns, jnp.asarray(first), jnp.asarray(second), pixels.reshape(tiles, 128),
        fractions.reshape(2, tiles, 128), own, jnp.asarray(forward), jnp.asarray(inverse),
    )
    f32, bf16 = jnp.float32, jnp.bfloat16
    smoothed, best = pl.pallas_call(
        functools.partial(kernel, size),
        out_shape=(
            jax.ShapeDtypeStruct((count, width), bf16),
            jax.ShapeDtypeStruct((count, 128), f32),
        ),
        in_specs=[pl.BlockSpec(memory_space=pl.ANY)] * 8,
        out_specs=(VMEM, VMEM),
        scratch_shapes=[pltpu.VMEM(x.shape, x.dtype) for x in operands]
        + [
            pltpu.VMEM((side, count, side), f32),
            pltpu.VMEM((side * count, side), bf16),
            pltpu.VMEM((side, CHUNK), bf16),
            pltpu.VMEM((side, CHUNK), bf16),
            pltpu.VMEM((tiles, count, 128), f32),
            pltpu.VMEM((RADII * count, WIDE), f32),
            pltpu.VMEM((RADII * count, 2 * HALF), f32),
            pltpu.VMEM((size * RADII, 2 * HALF), f32),
            pltpu.VMEM((size * count, 2 * HALF), f32),
            pltpu.VMEM((size, RADII, WIDE), bf16),
        ]
        + [pltpu.VMEM((tiles, 128), f32)] * 4
        + [
            pltpu.SemaphoreType.DMA((8,)),
            pltpu.SemaphoreType.DMA((size,)),
            pltpu.SemaphoreType.DMA((size,)),
            pltpu.SemaphoreType.DMA((2,)),
            pltpu.SemaphoreType.DMA((2,)),
        ],
        compiler_params=pltpu.CompilerParams(
            vmem_limit_bytes=56 << 20, collective_id=0, has_side_effects=True
        ),
        cost_estimate=pl.CostEstimate(
            flops=2 * count * side * side * width, bytes_accessed=4 << 20, transcendentals=0
        ),
    )(*operands)
    return smoothed, best[:, 0]


def solution(mesh):
    in_specs = (P(("groups", "corr"), None, None), P("corr", None), P(), P())
    out_specs = (P(("groups", "corr"), None), P(("groups", "corr")))
    return jax.shard_map(body, mesh=mesh, in_specs=in_specs, out_specs=out_specs, check_vma=False)
```

```python
import functools
import math

import jax
import jax.numpy as jnp
import ml_dtypes
import numpy as np
from jax import lax
from jax.experimental import pallas as pl
from jax.experimental.pallas import tpu as pltpu
from jax.sharding import PartitionSpec as P

RADII = 64
ANGLES = 360
FREQ = 181
SIGMA = 1.5
WIDE = 384
HALF = 256
CHUNK = 768
GROUP = 4
VMEM = pl.BlockSpec(memory_space=pltpu.VMEM)


def filter_tables(size):
    ids = np.arange(size)
    squared = ((ids[:, None] - ids[None, :]) ** 2).astype(np.float32)
    bell = np.exp(-squared / np.float32(2 * SIGMA**2)) / np.float32(math.sqrt(2 * math.pi) * SIGMA)
    curve = (squared / np.float32(SIGMA**4) - np.float32(1 / SIGMA**2)) * bell
    bell, curve = bell.astype(ml_dtypes.bfloat16), curve.astype(ml_dtypes.bfloat16)
    return np.concatenate([bell, curve], axis=1), np.concatenate([curve, bell], axis=1)


def dft_tables():
    phase = np.outer(np.arange(ANGLES), np.arange(FREQ)) % ANGLES * (2 * math.pi / ANGLES)
    forward = np.zeros((WIDE, 2 * HALF))
    forward[:ANGLES, :FREQ] = np.cos(phase)
    forward[:ANGLES, HALF : HALF + FREQ] = -np.sin(phase)
    factor = np.full((FREQ, 1), 2.0 / ANGLES)
    factor[0] = factor[FREQ - 1] = 1.0 / ANGLES
    inverse = np.zeros((2 * HALF, WIDE))
    inverse[:FREQ, :ANGLES] = np.cos(phase).T * factor
    inverse[HALF : HALF + FREQ, :ANGLES] = -np.sin(phase).T * factor
    inverse[:, ANGLES:] = inverse[:, :1]
    return forward.astype(ml_dtypes.bfloat16), inverse.astype(ml_dtypes.bfloat16)


def pick_tree(get, masks, level, at):
    if level == 0:
        return get(at)
    low = pick_tree(get, masks, level - 1, at)
    high = pick_tree(get, masks, level - 1, at + (1 << (level - 1)))
    return jnp.where(masks[level - 1], high, low)


def lanes_of(tile):
    return pl.ds(pl.multiple_of(tile * 128, 128), 128)


def column_weights(pix_ref, frac_ref, tile, side, out_ref):
    ids = lax.broadcasted_iota(jnp.int32, (side, 128), 0)
    for part in range(CHUNK // 128):
        col = pix_ref[pl.ds(tile + part, 1), :] & (side - 1)
        across = frac_ref[0:1, lanes_of(tile + part)]
        weights = jnp.where(ids == col, 1.0 - across, jnp.where(ids == col + 1, across, 0.0))
        out_ref[:, part * 128 : (part + 1) * 128] = weights.astype(jnp.bfloat16)


def sample_step(pix_ref, frac_ref, rows_ref, weights_ref, tile, count, bits):
    taken = jnp.dot(rows_ref[...], weights_ref[...], preferred_element_type=jnp.float32)
    out = []
    for part in range(CHUNK // 128):
        lanes = slice(part * 128, (part + 1) * 128)
        row = jnp.broadcast_to(pix_ref[pl.ds(tile + part, 1), :] >> (bits + 1), (count, 128))
        downward = jnp.broadcast_to(frac_ref[1:2, lanes_of(tile + part)], (count, 128))
        even_at, odd_at = (row + 1) >> 1, row >> 1
        even_masks = [(even_at & (1 << b)) != 0 for b in range(bits)]
        odd_masks = [(odd_at & (1 << b)) != 0 for b in range(bits)]

        def row_of(r):
            return taken[r * count : (r + 1) * count, lanes]

        even = pick_tree(lambda i: row_of(2 * i), even_masks, bits, 0)
        odd = pick_tree(lambda i: row_of(2 * i + 1), odd_masks, bits, 0)
        is_odd = (row & 1) != 0
        top = jnp.where(is_odd, odd, even)
        bottom = jnp.where(is_odd, even, odd)
        polar = (1.0 - downward) * top + downward * bottom
        out.append(polar.astype(jnp.bfloat16).astype(jnp.float32))
    return out


def kernel(
    size, pat_hbm, first_hbm, second_hbm, pix_hbm, frac_hbm, templ_hbm, fwd_hbm, inv_hbm,
    smooth_ref, best_ref,
    pat_ref, first_ref, second_ref, pix_ref, frac_ref, row_ref, fwd_ref, inv_ref,
    templ_ref, norm_ref, wide_ref, rows_ref, even_ref, odd_ref, padded_ref, line_ref, spec_ref, templ_spec_ref,
    cross_ref, library_ref, last_ref, first_row_ref, low_ref, high_ref,
    load_sem, send_sem, recv_sem, halo_send, halo_recv,
):
    me = lax.axis_index("corr")
    loads = [
        pltpu.make_async_copy(source, target, load_sem.at[i])
        for i, (source, target) in enumerate((
            (templ_hbm, row_ref), (pat_hbm, pat_ref), (first_hbm, first_ref),
            (second_hbm, second_ref), (pix_hbm, pix_ref), (frac_hbm, frac_ref),
            (fwd_hbm, fwd_ref), (inv_hbm, inv_ref),
        ))
    ]
    for load in loads:
        load.start()

    barrier = pltpu.get_barrier_semaphore()

    def partner(k):
        return {"corr": lax.rem(me + k, size)}

    @pl.loop(1, size)
    def _(k):
        pl.semaphore_signal(
            barrier, inc=1, device_id=partner(k), device_id_type=pl.DeviceIdType.MESH
        )

    def share(k):
        return pltpu.make_async_remote_copy(
            src_ref=templ_ref,
            dst_ref=library_ref.at[me],
            send_sem=send_sem.at[k],
            recv_sem=recv_sem.at[k],
            device_id=partner(k),
            device_id_type=pl.DeviceIdType.MESH,
        )

    count, side = pat_ref.shape[0], pat_ref.shape[1]
    bits = side.bit_length() - 2
    tiles = pix_ref.shape[0]
    width = tiles * 128
    for load in loads[1:4]:
        load.wait()
    for p in range(count):
        left = jnp.dot(pat_ref[p], first_ref[...], preferred_element_type=jnp.float32)
        left = left.astype(jnp.bfloat16)
        left = jnp.concatenate([left[:, :side], left[:, side:]], axis=0)
        filtered = jnp.dot(second_ref[...], left, preferred_element_type=jnp.float32)
        wide_ref[:, p, :] = filtered
    rows_ref[...] = wide_ref[...].reshape(side * count, side).astype(jnp.bfloat16)
    loads[0].wait()
    real_lane = lax.broadcasted_iota(jnp.int32, (1, WIDE), 1) < ANGLES
    row = row_ref[...].astype(jnp.float32)
    for r in range(RADII):
        start = r * ANGLES
        base = min(start // 128, tiles - 4)
        window = row[:, base * 128 : base * 128 + 512]
        if start > base * 128:
            window = pltpu.roll(window, 512 - (start - base * 128), 1)
        line_ref[r : r + 1, :] = jnp.where(real_lane, window[:, :WIDE], 0.0)
    templ_ref[...] = line_ref[0:RADII, :].astype(jnp.bfloat16)
    pl.semaphore_wait(barrier, size - 1)

    @pl.loop(1, size)
    def _(k):
        share(k).start()

    library_ref[me] = templ_ref[...]

    loads[4].wait()
    loads[5].wait()

    each = CHUNK // 128
    pairs = tiles // (2 * each)
    column_weights(pix_ref, frac_ref, 0, side, even_ref)

    def keep(tile, rows):
        for part, polar in enumerate(rows):
            padded_ref[tile + part] = polar
            first_row_ref[pl.ds(tile + part, 1), :] = polar[:1]
            last_ref[pl.ds(tile + part, 1), :] = polar[count - 1 :]

    @pl.loop(0, pairs)
    def _(step):
        now = step * (2 * each)
        later = lax.rem(step + 1, pairs) * (2 * each)
        column_weights(pix_ref, frac_ref, now + each, side, odd_ref)
        rows = sample_step(pix_ref, frac_ref, rows_ref, even_ref, now, count, bits)
        column_weights(pix_ref, frac_ref, later, side, even_ref)
        more = sample_step(pix_ref, frac_ref, rows_ref, odd_ref, now + each, count, bits)
        keep(now, rows)
        keep(now + each, more)

    def halo(i, source, target, to):
        return pltpu.make_async_remote_copy(
            src_ref=source,
            dst_ref=target,
            send_sem=halo_send.at[i],
            recv_sem=halo_recv.at[i],
            device_id={"corr": to},
            device_id_type=pl.DeviceIdType.MESH,
        )

    upward = halo(0, last_ref, low_ref, lax.rem(me + 1, size))
    downward = halo(1, first_row_ref, high_ref, lax.rem(me + size - 1, size))
    upward.start()
    downward.start()
    loads[6].wait()
    loads[7].wait()

    @pl.loop(1, size)
    def _(k):
        share(k).wait()

    def spectrum(lines):
        return jnp.dot(lines, fwd_ref[...], preferred_element_type=jnp.float32)

    @pl.loop(0, size // GROUP)
    def _(group):
        lines = library_ref[pl.ds(group * GROUP, GROUP)].reshape(GROUP * RADII, WIDE)
        at = pl.ds(pl.multiple_of(group * (GROUP * RADII), GROUP * RADII), GROUP * RADII)
        templ_spec_ref[at, :] = spectrum(lines)
        lines = lines.astype(jnp.float32)
        squares = lines * lines
        squares = squares[:, :128] + squares[:, 128:256] + squares[:, 256:]
        for i in range(GROUP):
            part = jnp.sum(squares[i * RADII : (i + 1) * RADII], axis=0, keepdims=True)
            out = pl.ds(pl.multiple_of((group * GROUP + i) * count, count), count)
            norm_ref[out, :] = jnp.broadcast_to(part, (count, 128))

    upward.wait()
    downward.wait()
    has_low = jnp.where(me > 0, 1.0, 0.0)
    has_high = jnp.where(me < size - 1, 1.0, 0.0)
    ids = lax.broadcasted_iota(jnp.int32, (count, 128), 0)
    total = jnp.zeros((count, 128), jnp.float32)
    for tile in range(tiles):
        rows = padded_ref[tile]
        low = jnp.broadcast_to(low_ref[tile : tile + 1, :], rows.shape) * has_low
        high = jnp.broadcast_to(high_ref[tile : tile + 1, :], rows.shape) * has_high
        before = jnp.where(ids == 0, low, pltpu.roll(rows, 1, 0))
        after = jnp.where(ids == count - 1, high, pltpu.roll(rows, count - 1, 0))
        smooth = ((before + 2.0 * rows + after) * 0.25).astype(jnp.bfloat16)
        smooth_ref[:, tile * 128 : (tile + 1) * 128] = smooth
        smooth = smooth.astype(jnp.float32)
        padded_ref[tile] = smooth
        total = total + smooth * smooth
    pattern_norm = jnp.sqrt(jnp.sum(total, axis=1, keepdims=True) + 1e-06)

    real_lane = lax.broadcasted_iota(jnp.int32, (count, WIDE), 1) < ANGLES
    for r in range(RADII):
        start = r * ANGLES
        base = start // 128
        window = jnp.concatenate([padded_ref[min(base + i, tiles - 1)] for i in range(4)], axis=1)
        if start > base * 128:
            window = pltpu.roll(window, 512 - (start - base * 128), 1)
        line_ref[r * count : (r + 1) * count, :] = jnp.where(real_lane, window[:, :WIDE], 0.0)
    spec_ref[...] = spectrum(line_ref[...].astype(jnp.bfloat16))

    @pl.loop(0, size // GROUP)
    def _(group):
        zero = jnp.zeros((count, HALF), jnp.float32)
        real, imag = [zero] * GROUP, [zero] * GROUP
        for r in range(RADII):
            pat = spec_ref[r * count : (r + 1) * count, :]
            pr, pi = pat[:, :HALF], pat[:, HALF:]
            for i in range(GROUP):
                tem = templ_spec_ref[pl.ds((group * GROUP + i) * RADII + r, 1), :]
                tr, ti = tem[:, :HALF], tem[:, HALF:]
                real[i] = real[i] + pr * tr + pi * ti
                imag[i] = imag[i] + pr * ti - pi * tr
        for i in range(GROUP):
            out = pl.ds(pl.multiple_of((group * GROUP + i) * count, count), count)
            cross_ref[out, :HALF] = real[i]
            cross_ref[out, HALF:] = imag[i]

    shifted = jnp.dot(
        cross_ref[...].astype(jnp.bfloat16), inv_ref[...], preferred_element_type=jnp.float32
    )
    shifted = jnp.maximum(jnp.maximum(shifted[:, :128], shifted[:, 128:256]), shifted[:, 256:])
    norm = jnp.sqrt(jnp.sum(norm_ref[...], axis=1, keepdims=True) + 1e-06)
    scaled = jnp.max(shifted, axis=1, keepdims=True) / norm
    scaled = jnp.broadcast_to(scaled, (size * count, 128)).reshape(size, count, 128)
    best = jnp.max(scaled, axis=0) * math.sqrt(RADII * ANGLES) / pattern_norm
    diagonal = ids == lax.broadcasted_iota(jnp.int32, (count, 128), 1)
    best_ref[...] = jnp.sum(jnp.where(diagonal, best, 0.0), axis=0, keepdims=True)[:, :count]


def body(patterns, templates, pixels, fractions):
    count, side = patterns.shape[0], patterns.shape[1]
    width = pixels.shape[0]
    tiles = width // 128
    first, second = filter_tables(side)
    forward, inverse = dft_tables()
    size = lax.axis_size("corr")
    operands = (
        patterns, jnp.asarray(first), jnp.asarray(second), pixels.reshape(tiles, 128),
        fractions, templates, jnp.asarray(forward), jnp.asarray(inverse),
    )
    f32, bf16 = jnp.float32, jnp.bfloat16
    smoothed, best = pl.pallas_call(
        functools.partial(kernel, size),
        out_shape=(
            jax.ShapeDtypeStruct((count, width), bf16),
            jax.ShapeDtypeStruct((1, count), f32),
        ),
        in_specs=[pl.BlockSpec(memory_space=pl.ANY)] * 8,
        out_specs=(VMEM, VMEM),
        scratch_shapes=[pltpu.VMEM(x.shape, x.dtype) for x in operands]
        + [
            pltpu.VMEM((RADII, WIDE), bf16),
            pltpu.VMEM((size * count, 128), f32),
            pltpu.VMEM((side, count, side), f32),
            pltpu.VMEM((side * count, side), bf16),
            pltpu.VMEM((side, CHUNK), bf16),
            pltpu.VMEM((side, CHUNK), bf16),
            pltpu.VMEM((tiles, count, 128), f32),
            pltpu.VMEM((RADII * count, WIDE), f32),
            pltpu.VMEM((RADII * count, 2 * HALF), f32),
            pltpu.VMEM((size * RADII, 2 * HALF), f32),
            pltpu.VMEM((size * count, 2 * HALF), f32),
            pltpu.VMEM((size, RADII, WIDE), bf16),
        ]
        + [pltpu.VMEM((tiles, 128), f32)] * 4
        + [
            pltpu.SemaphoreType.DMA((8,)),
            pltpu.SemaphoreType.DMA((size,)),
            pltpu.SemaphoreType.DMA((size,)),
            pltpu.SemaphoreType.DMA((2,)),
            pltpu.SemaphoreType.DMA((2,)),
        ],
        compiler_params=pltpu.CompilerParams(
            vmem_limit_bytes=56 << 20, collective_id=0, has_side_effects=True
        ),
        cost_estimate=pl.CostEstimate(
            flops=2 * count * side * side * width, bytes_accessed=4 << 20, transcendentals=0
        ),
    )(*operands)
    return smoothed, best.reshape(count)


def solution(mesh):
    in_specs = (P(("groups", "corr"), None, None), P("corr", None), P(), P())
    out_specs = (P(("groups", "corr"), None), P(("groups", "corr")))
    return jax.shard_map(body, mesh=mesh, in_specs=in_specs, out_specs=out_specs, check_vma=False)
```

```python
import functools
import math

import jax
import jax.numpy as jnp
import ml_dtypes
import numpy as np
from jax import lax
from jax.experimental import pallas as pl
from jax.experimental.pallas import tpu as pltpu
from jax.sharding import PartitionSpec as P

RADII = 64
ANGLES = 360
FREQ = 181
SIGMA = 1.5
WIDE = 384
HALF = 256
CHUNK = 1280
GROUP = 4
VMEM = pl.BlockSpec(memory_space=pltpu.VMEM)


def filter_tables(size):
    ids = np.arange(size)
    squared = ((ids[:, None] - ids[None, :]) ** 2).astype(np.float32)
    bell = np.exp(-squared / np.float32(2 * SIGMA**2)) / np.float32(math.sqrt(2 * math.pi) * SIGMA)
    curve = (squared / np.float32(SIGMA**4) - np.float32(1 / SIGMA**2)) * bell
    bell, curve = bell.astype(ml_dtypes.bfloat16), curve.astype(ml_dtypes.bfloat16)
    return np.concatenate([bell, curve], axis=1), np.concatenate([curve, bell], axis=1)


def dft_tables():
    phase = np.outer(np.arange(ANGLES), np.arange(FREQ)) % ANGLES * (2 * math.pi / ANGLES)
    forward = np.zeros((WIDE, 2 * HALF))
    forward[:ANGLES, :FREQ] = np.cos(phase)
    forward[:ANGLES, HALF : HALF + FREQ] = -np.sin(phase)
    factor = np.full((FREQ, 1), 2.0 / ANGLES)
    factor[0] = factor[FREQ - 1] = 1.0 / ANGLES
    inverse = np.zeros((2 * HALF, WIDE))
    inverse[:FREQ, :ANGLES] = np.cos(phase).T * factor
    inverse[HALF : HALF + FREQ, :ANGLES] = -np.sin(phase).T * factor
    inverse[:, ANGLES:] = inverse[:, :1]
    return forward.astype(ml_dtypes.bfloat16), inverse.astype(ml_dtypes.bfloat16)


def pick_tree(get, masks, level, at):
    if level == 0:
        return get(at)
    low = pick_tree(get, masks, level - 1, at)
    high = pick_tree(get, masks, level - 1, at + (1 << (level - 1)))
    return jnp.where(masks[level - 1], high, low)


def lanes_of(tile):
    return pl.ds(pl.multiple_of(tile * 128, 128), 128)


def column_weights(pix_ref, frac_ref, tile, side, out_ref):
    ids = lax.broadcasted_iota(jnp.int32, (side, 128), 0)
    for part in range(CHUNK // 128):
        col = pix_ref[pl.ds(tile + part, 1), :] & (side - 1)
        across = frac_ref[0:1, lanes_of(tile + part)]
        weights = jnp.where(ids == col, 1.0 - across, jnp.where(ids == col + 1, across, 0.0))
        out_ref[:, part * 128 : (part + 1) * 128] = weights.astype(jnp.bfloat16)


def sample_step(pix_ref, frac_ref, rows_ref, weights_ref, tile, count, bits):
    block = rows_ref.shape[0] // count
    taken = jnp.concatenate(
        [
            jnp.dot(
                rows_ref[i * block : (i + 1) * block, :], weights_ref[...],
                preferred_element_type=jnp.float32,
            )
            for i in range(count)
        ],
        axis=0,
    )
    out = []
    for part in range(CHUNK // 128):
        lanes = slice(part * 128, (part + 1) * 128)
        row = jnp.broadcast_to(pix_ref[pl.ds(tile + part, 1), :] >> (bits + 1), (count, 128))
        downward = jnp.broadcast_to(frac_ref[1:2, lanes_of(tile + part)], (count, 128))
        even_at, odd_at = (row + 1) >> 1, row >> 1
        even_masks = [(even_at & (1 << b)) != 0 for b in range(bits)]
        odd_masks = [(odd_at & (1 << b)) != 0 for b in range(bits)]

        def row_of(r):
            return taken[r * count : (r + 1) * count, lanes]

        even = pick_tree(lambda i: row_of(2 * i), even_masks, bits, 0)
        odd = pick_tree(lambda i: row_of(2 * i + 1), odd_masks, bits, 0)
        is_odd = (row & 1) != 0
        top = jnp.where(is_odd, odd, even)
        bottom = jnp.where(is_odd, even, odd)
        polar = (1.0 - downward) * top + downward * bottom
        out.append(polar.astype(jnp.bfloat16).astype(jnp.float32))
    return out


def kernel(
    size, pat_hbm, first_hbm, second_hbm, pix_hbm, frac_hbm, templ_hbm, fwd_hbm, inv_hbm,
    smooth_ref, best_ref,
    pat_ref, first_ref, second_ref, pix_ref, frac_ref, row_ref, fwd_ref, inv_ref,
    templ_ref, norm_ref, wide_ref, rows_ref, even_ref, odd_ref, padded_ref, line_ref, spec_ref, templ_spec_ref,
    cross_ref, library_ref, last_ref, first_row_ref, low_ref, high_ref,
    load_sem, send_sem, recv_sem, halo_send, halo_recv,
):
    me = lax.axis_index("corr")
    loads = [
        pltpu.make_async_copy(source, target, load_sem.at[i])
        for i, (source, target) in enumerate((
            (templ_hbm, row_ref), (pat_hbm, pat_ref), (first_hbm, first_ref),
            (second_hbm, second_ref), (pix_hbm, pix_ref), (frac_hbm, frac_ref),
            (fwd_hbm, fwd_ref), (inv_hbm, inv_ref),
        ))
    ]
    for load in loads:
        load.start()

    barrier = pltpu.get_barrier_semaphore()

    def partner(k):
        return {"corr": lax.rem(me + k, size)}

    @pl.loop(1, size)
    def _(k):
        pl.semaphore_signal(
            barrier, inc=1, device_id=partner(k), device_id_type=pl.DeviceIdType.MESH
        )

    def share(k):
        return pltpu.make_async_remote_copy(
            src_ref=templ_ref,
            dst_ref=library_ref.at[me],
            send_sem=send_sem.at[k],
            recv_sem=recv_sem.at[k],
            device_id=partner(k),
            device_id_type=pl.DeviceIdType.MESH,
        )

    count, side = pat_ref.shape[0], pat_ref.shape[1]
    bits = side.bit_length() - 2
    tiles = pix_ref.shape[0]
    width = tiles * 128
    for load in loads[1:4]:
        load.wait()
    for p in range(count):
        left = jnp.dot(pat_ref[p], first_ref[...], preferred_element_type=jnp.float32)
        left = left.astype(jnp.bfloat16)
        left = jnp.concatenate([left[:, :side], left[:, side:]], axis=0)
        filtered = jnp.dot(second_ref[...], left, preferred_element_type=jnp.float32)
        wide_ref[:, p, :] = filtered
    rows_ref[...] = wide_ref[...].reshape(side * count, side).astype(jnp.bfloat16)
    loads[0].wait()
    real_lane = lax.broadcasted_iota(jnp.int32, (1, WIDE), 1) < ANGLES
    row = row_ref[...].astype(jnp.float32)
    for r in range(RADII):
        start = r * ANGLES
        base = min(start // 128, tiles - 4)
        window = row[:, base * 128 : base * 128 + 512]
        if start > base * 128:
            window = pltpu.roll(window, 512 - (start - base * 128), 1)
        line_ref[r : r + 1, :] = jnp.where(real_lane, window[:, :WIDE], 0.0)
    templ_ref[...] = line_ref[0:RADII, :].astype(jnp.bfloat16)
    pl.semaphore_wait(barrier, size - 1)

    @pl.loop(1, size)
    def _(k):
        share(k).start()

    library_ref[me] = templ_ref[...]

    loads[4].wait()
    loads[5].wait()

    each = CHUNK // 128
    pairs = tiles // (2 * each)
    column_weights(pix_ref, frac_ref, 0, side, even_ref)

    def keep(tile, rows):
        for part, polar in enumerate(rows):
            padded_ref[tile + part] = polar
            first_row_ref[pl.ds(tile + part, 1), :] = polar[:1]
            last_ref[pl.ds(tile + part, 1), :] = polar[count - 1 :]

    @pl.loop(0, pairs)
    def _(step):
        now = step * (2 * each)
        later = lax.rem(step + 1, pairs) * (2 * each)
        column_weights(pix_ref, frac_ref, now + each, side, odd_ref)
        rows = sample_step(pix_ref, frac_ref, rows_ref, even_ref, now, count, bits)
        column_weights(pix_ref, frac_ref, later, side, even_ref)
        more = sample_step(pix_ref, frac_ref, rows_ref, odd_ref, now + each, count, bits)
        keep(now, rows)
        keep(now + each, more)

    def halo(i, source, target, to):
        return pltpu.make_async_remote_copy(
            src_ref=source,
            dst_ref=target,
            send_sem=halo_send.at[i],
            recv_sem=halo_recv.at[i],
            device_id={"corr": to},
            device_id_type=pl.DeviceIdType.MESH,
        )

    upward = halo(0, last_ref, low_ref, lax.rem(me + 1, size))
    downward = halo(1, first_row_ref, high_ref, lax.rem(me + size - 1, size))
    upward.start()
    downward.start()
    loads[6].wait()
    loads[7].wait()

    @pl.loop(1, size)
    def _(k):
        share(k).wait()

    def spectrum(lines):
        return jnp.dot(lines, fwd_ref[...], preferred_element_type=jnp.float32)

    @pl.loop(0, size // GROUP)
    def _(group):
        lines = library_ref[pl.ds(group * GROUP, GROUP)].reshape(GROUP * RADII, WIDE)
        at = pl.ds(pl.multiple_of(group * (GROUP * RADII), GROUP * RADII), GROUP * RADII)
        templ_spec_ref[at, :] = spectrum(lines)
        lines = lines.astype(jnp.float32)
        squares = lines * lines
        squares = squares[:, :128] + squares[:, 128:256] + squares[:, 256:]
        for i in range(GROUP):
            part = jnp.sum(squares[i * RADII : (i + 1) * RADII], axis=0, keepdims=True)
            out = pl.ds(pl.multiple_of((group * GROUP + i) * count, count), count)
            norm_ref[out, :] = jnp.broadcast_to(part, (count, 128))

    upward.wait()
    downward.wait()
    has_low = jnp.where(me > 0, 1.0, 0.0)
    has_high = jnp.where(me < size - 1, 1.0, 0.0)
    ids = lax.broadcasted_iota(jnp.int32, (count, 128), 0)
    total = jnp.zeros((count, 128), jnp.float32)
    for tile in range(tiles):
        rows = padded_ref[tile]
        low = jnp.broadcast_to(low_ref[tile : tile + 1, :], rows.shape) * has_low
        high = jnp.broadcast_to(high_ref[tile : tile + 1, :], rows.shape) * has_high
        before = jnp.where(ids == 0, low, pltpu.roll(rows, 1, 0))
        after = jnp.where(ids == count - 1, high, pltpu.roll(rows, count - 1, 0))
        smooth = ((before + 2.0 * rows + after) * 0.25).astype(jnp.bfloat16)
        smooth_ref[:, tile * 128 : (tile + 1) * 128] = smooth
        smooth = smooth.astype(jnp.float32)
        padded_ref[tile] = smooth
        total = total + smooth * smooth
    pattern_norm = jnp.sqrt(jnp.sum(total, axis=1, keepdims=True) + 1e-06)

    real_lane = lax.broadcasted_iota(jnp.int32, (count, WIDE), 1) < ANGLES
    for r in range(RADII):
        start = r * ANGLES
        base = start // 128
        window = jnp.concatenate([padded_ref[min(base + i, tiles - 1)] for i in range(4)], axis=1)
        if start > base * 128:
            window = pltpu.roll(window, 512 - (start - base * 128), 1)
        line_ref[r * count : (r + 1) * count, :] = jnp.where(real_lane, window[:, :WIDE], 0.0)
    spec_ref[...] = spectrum(line_ref[...].astype(jnp.bfloat16))

    @pl.loop(0, size // GROUP)
    def _(group):
        zero = jnp.zeros((count, HALF), jnp.float32)
        real, imag = [zero] * GROUP, [zero] * GROUP
        for r in range(RADII):
            pat = spec_ref[r * count : (r + 1) * count, :]
            pr, pi = pat[:, :HALF], pat[:, HALF:]
            for i in range(GROUP):
                tem = templ_spec_ref[pl.ds((group * GROUP + i) * RADII + r, 1), :]
                tr, ti = tem[:, :HALF], tem[:, HALF:]
                real[i] = real[i] + pr * tr + pi * ti
                imag[i] = imag[i] + pr * ti - pi * tr
        for i in range(GROUP):
            out = pl.ds(pl.multiple_of((group * GROUP + i) * count, count), count)
            cross_ref[out, :HALF] = real[i]
            cross_ref[out, HALF:] = imag[i]

    shifted = jnp.dot(
        cross_ref[...].astype(jnp.bfloat16), inv_ref[...], preferred_element_type=jnp.float32
    )
    shifted = jnp.maximum(jnp.maximum(shifted[:, :128], shifted[:, 128:256]), shifted[:, 256:])
    norm = jnp.sqrt(jnp.sum(norm_ref[...], axis=1, keepdims=True) + 1e-06)
    scaled = jnp.max(shifted, axis=1, keepdims=True) / norm
    scaled = jnp.broadcast_to(scaled, (size * count, 128)).reshape(size, count, 128)
    best = jnp.max(scaled, axis=0) * math.sqrt(RADII * ANGLES) / pattern_norm
    diagonal = ids == lax.broadcasted_iota(jnp.int32, (count, 128), 1)
    best_ref[...] = jnp.sum(jnp.where(diagonal, best, 0.0), axis=0, keepdims=True)[:, :count]


def body(patterns, templates, pixels, fractions):
    count, side = patterns.shape[0], patterns.shape[1]
    width = pixels.shape[0]
    tiles = width // 128
    first, second = filter_tables(side)
    forward, inverse = dft_tables()
    size = lax.axis_size("corr")
    operands = (
        patterns, jnp.asarray(first), jnp.asarray(second), pixels.reshape(tiles, 128),
        fractions, templates, jnp.asarray(forward), jnp.asarray(inverse),
    )
    f32, bf16 = jnp.float32, jnp.bfloat16
    smoothed, best = pl.pallas_call(
        functools.partial(kernel, size),
        out_shape=(
            jax.ShapeDtypeStruct((count, width), bf16),
            jax.ShapeDtypeStruct((1, count), f32),
        ),
        in_specs=[pl.BlockSpec(memory_space=pl.ANY)] * 8,
        out_specs=(VMEM, VMEM),
        scratch_shapes=[pltpu.VMEM(x.shape, x.dtype) for x in operands]
        + [
            pltpu.VMEM((RADII, WIDE), bf16),
            pltpu.VMEM((size * count, 128), f32),
            pltpu.VMEM((side, count, side), f32),
            pltpu.VMEM((side * count, side), bf16),
            pltpu.VMEM((side, CHUNK), bf16),
            pltpu.VMEM((side, CHUNK), bf16),
            pltpu.VMEM((tiles, count, 128), f32),
            pltpu.VMEM((RADII * count, WIDE), f32),
            pltpu.VMEM((RADII * count, 2 * HALF), f32),
            pltpu.VMEM((size * RADII, 2 * HALF), f32),
            pltpu.VMEM((size * count, 2 * HALF), f32),
            pltpu.VMEM((size, RADII, WIDE), bf16),
        ]
        + [pltpu.VMEM((tiles, 128), f32)] * 4
        + [
            pltpu.SemaphoreType.DMA((8,)),
            pltpu.SemaphoreType.DMA((size,)),
            pltpu.SemaphoreType.DMA((size,)),
            pltpu.SemaphoreType.DMA((2,)),
            pltpu.SemaphoreType.DMA((2,)),
        ],
        compiler_params=pltpu.CompilerParams(
            vmem_limit_bytes=56 << 20, collective_id=0, has_side_effects=True
        ),
        cost_estimate=pl.CostEstimate(
            flops=2 * count * side * side * width, bytes_accessed=4 << 20, transcendentals=0
        ),
    )(*operands)
    return smoothed, best.reshape(count)


def solution(mesh):
    in_specs = (P(("groups", "corr"), None, None), P("corr", None), P(), P())
    out_specs = (P(("groups", "corr"), None), P(("groups", "corr")))
    return jax.shard_map(body, mesh=mesh, in_specs=in_specs, out_specs=out_specs, check_vma=False)
```
